32 devices in a mesh: groups: 2 (over y), wide: 4 (over x, core), narrow: 4 (over z).
Axes of the slice: x: 2, y: 2, z: 4, core: 2. Of those that a mesh axis runs over, the one named last changes fastest.
Arguments:
- coords: bfloat16 [256, 3, 256], P(('groups', 'wide', 'narrow')), parts along dimension 0, may hold values from 0 to 1
- probe: float32 [256, 8, 256], P(('groups', 'wide', 'narrow')), parts along dimension 0
- kept: float32 [256, 8, 256], P(('groups', 'wide', 'narrow')), parts along dimension 0
- pairs: int32 [8, 4, 64, 2], P(('groups', 'wide'), 'narrow'), parts along dimension 0, may hold values from 0 to 11, as said below
- counts: int32 [8, 4], P(('groups', 'wide'), 'narrow'), parts along dimension 0, may hold values from 16 to 64, as said below
- send_list: int32 [8, 4, 4, 6], P(('groups', 'wide'), 'narrow'), parts along dimension 0, may hold values from 0 to 7
- target_list: int32 [8, 4, 4, 6], P(('groups', 'wide'), 'narrow'), parts along dimension 0, may hold values from 0 to 7
Outputs:
- next_block: float32 [256, 8, 256], P(('groups', 'wide', 'narrow')), parts along dimension 0
- projections: float32 [32, 8], P('groups'), parts along dimension 0
The draws below stay inside these ranges and needn't reach their ends.
There are 2 independent parts, one for each index of `groups`. The reference program is written for one: setup_inputs(seed, part) draws one part's arguments, and reference() takes and returns one part's arrays. A program takes and returns all parts, laid end to end along the dimension named above; each array names one. Nothing has to cross between parts.
Inputs may be any that keep to these rules, and one draw needn't show every extreme that they name: The pairs of one device are distinct; column slots lie in 0 to 11, row blocks in 0 to 7. `counts`: some device has 64 live pairs.
All inputs are finite; a program needn't handle non-finite values.
Results may differ from the reference program's by a relative error of at most 0.0038.
Values may be sent and summed in bfloat16 or wider, within the bound.
A program may use at most 64 MiB of HBM per device.

```python
import jax
import jax.numpy as jnp
from jax import lax

NB = 8
BS = 256
PROBES = 8
KEPT = 8
HALO = 2
SLOTS = 6
PAIRS = 64
BLOCKS = 128
SITES = 32768
N_WIDE = 4
N_NARROW = 4


def morton_cells():
    index = jnp.arange(BLOCKS, dtype=jnp.int32)
    level_bits = BLOCKS.bit_length() - 1
    places = [jnp.zeros((BLOCKS,), jnp.int32) for axis_index in range(3)]
    extents = [1, 1, 1]
    for bit_index in range(level_bits):
        axis_index = bit_index % 3
        bit_value = index // 2 ** bit_index % 2
        places[axis_index] = places[axis_index] + bit_value * extents[axis_index]
        extents[axis_index] = extents[axis_index] * 2
    return (places, extents)


def far_choice(key):
    key = jax.random.fold_in(key, 41)
    places, extents = morton_cells()
    largest = max(extents)
    scaled = jnp.stack([(2 * places[k] + 1) * (largest // extents[k]) for k in range(3)], axis=-1)
    blocked = scaled.reshape(N_WIDE, N_NARROW, NB, 3)
    sources = jnp.transpose(blocked, (1, 0, 2, 3))
    offset = blocked[:, :, None, :, None, :] - sources[None, :, :, None, :, :]
    distance = jnp.sum(offset * offset, axis=-1)
    groups_total = N_WIDE * N_NARROW * N_WIDE
    keys = jax.random.split(key, groups_total)
    ranks = jax.vmap(lambda k: jax.random.permutation(k, NB * NB))(keys)
    ranks = ranks.reshape(N_WIDE, N_NARROW, N_WIDE, NB * NB).astype(jnp.int32)
    score = distance.reshape(N_WIDE, N_NARROW, N_WIDE, NB * NB) * (NB * NB) + ranks
    order = jnp.argsort(score, axis=-1, stable=True)[..., :SLOTS].astype(jnp.int32)
    rows = order // NB
    sent = order % NB
    rows = rows.at[0, 0, 0, 0].set(NB - 1).at[0, 0, 1, 0].set(0)
    sent = sent.at[0, 0, 0, 0].set(0).at[0, 0, 1, 0].set(NB - 1)
    return (rows, sent)


def draw_target_list(key, part):
    rows, sent = far_choice(key)
    return rows.astype(jnp.int32)


def draw_send_list(key, part):
    rows, sent = far_choice(key)
    return jnp.transpose(sent, (2, 1, 0, 3)).astype(jnp.int32)


def draw_coords(key, part):
    key = jax.random.fold_in(key, 51)
    places, extents = morton_cells()
    centres = jnp.stack([(places[k].astype(jnp.float32) + 0.5) / extents[k] for k in range(3)], axis=1)
    widths = jnp.array([1.0 / extents[k] for k in range(3)], jnp.float32)
    jitter = jax.random.uniform(key, (BLOCKS, 3, BS), jnp.float32, -0.5, 0.5)
    sites = centres[:, :, None] + jitter * widths[None, :, None]
    return jnp.clip(sites, 0.0, 1.0).astype(jnp.bfloat16)


def shared_normal(key):
    return jax.random.normal(key, (BLOCKS, KEPT, BS), jnp.float32)


def draw_kept(key, part):
    shared = shared_normal(key)
    return shared


def draw_probe(key, part):
    shared = shared_normal(key)
    key = jax.random.fold_in(key, 12)
    mixed_in = jnp.roll(shared, 3, axis=1)[:, :PROBES, :]
    noise = 0.8 * jax.random.normal(key, (BLOCKS, PROBES, BS), jnp.float32)
    return 0.6 * mixed_in + noise


def draw_pairs(key, part):
    key = jax.random.fold_in(key, 21)
    span = NB + 2 * HALO
    tiles = NB * span
    keys = jax.random.split(key, N_WIDE * N_NARROW)
    shuffled = jax.vmap(lambda k: jax.random.permutation(k, tiles))(keys).astype(jnp.int32)
    first = shuffled[0]
    where_last = jnp.argmax(first == span - 1)
    shuffled = shuffled.at[0].set(jnp.roll(first, -where_last))
    chosen = shuffled[:, :PAIRS].reshape(N_WIDE, N_NARROW, PAIRS)
    pair_rows = chosen // span
    pair_slots = chosen % span
    return jnp.stack([pair_rows, pair_slots], axis=-1).astype(jnp.int32)


def draw_counts(key, part):
    key = jax.random.fold_in(key, 31)
    first_key, second_key = jax.random.split(key)
    lowest = max(PAIRS // 4, 1)
    drawn = jax.random.randint(first_key, (N_WIDE * N_NARROW,), lowest, PAIRS + 1)
    chosen = jax.random.permutation(second_key, N_WIDE * N_NARROW)
    drawn = drawn.at[chosen[0]].set(PAIRS).at[chosen[1]].set(lowest)
    return drawn.reshape(N_WIDE, N_NARROW).astype(jnp.int32)


def setup_inputs(seed: int = 0, part: int = 0) -> dict:
    key_of = jax.random.split(jax.random.key(seed), 8)
    part_keys = jax.random.split(jax.random.fold_in(key_of[7], part), 8)
    coords = draw_coords(jax.random.fold_in(jax.random.fold_in(key_of[7], part), 71), part)
    probe = draw_probe(jax.random.fold_in(jax.random.fold_in(key_of[7], part), 71), part)
    kept = draw_kept(jax.random.fold_in(jax.random.fold_in(key_of[7], part), 71), part)
    pairs = draw_pairs(jax.random.fold_in(jax.random.fold_in(key_of[7], part), 71), part)
    counts = draw_counts(jax.random.fold_in(jax.random.fold_in(key_of[7], part), 71), part)
    send_list = draw_send_list(jax.random.fold_in(jax.random.fold_in(key_of[7], part), 71), part)
    target_list = draw_target_list(jax.random.fold_in(jax.random.fold_in(key_of[7], part), 71), part)
    return dict(coords=coords, probe=probe, kept=kept, pairs=pairs, counts=counts, send_list=send_list, target_list=target_list)


rho = 0.35
signal = 0.25
nugget = 1.0
eps = 1e-06

def tile_product(row_sites, col_sites, col_probe):
    row_float = row_sites.astype(jnp.float32)
    col_float = col_sites.astype(jnp.float32)
    squared = None
    for component in range(3):
        offset = row_float[..., component, :, None] - col_float[..., component, None, :]
        squared = offset * offset if squared is None else squared + offset * offset
    scaled = jnp.sqrt(squared) / rho
    support = jnp.maximum(1.0 - scaled, 0.0)
    quartic = support * support * (support * support)
    kernel_tile = (signal * quartic * (4.0 * scaled + 1.0)).astype(jnp.bfloat16)
    return jnp.einsum('...cj,...ij->...ci', col_probe.astype(jnp.float32), kernel_tile.astype(jnp.float32))

def reference(coords, probe, kept, pairs, counts, send_list, target_list):
    probe_half = probe.astype(jnp.bfloat16)

    def per_device(device):
        wide_index = device // N_NARROW
        narrow_index = device % N_NARROW
        own_sites = lax.dynamic_slice_in_dim(coords, device * NB, NB, 0)
        pair_list = pairs[wide_index, narrow_index]
        pair_rows = pair_list[:, 0]
        pair_slots = pair_list[:, 1]
        within = narrow_index * NB - HALO + pair_slots
        valid = (within >= 0) & (within < N_NARROW * NB)
        column = jnp.clip(device * NB - HALO + pair_slots, 0, BLOCKS - 1)
        active = (jnp.arange(PAIRS) < counts[wide_index, narrow_index]) & valid
        local_terms = tile_product(own_sites[pair_rows], coords[column], probe_half[column])
        local_terms = jnp.where(active[:, None, None], local_terms, jnp.float32(0.0))
        summed = jnp.zeros((NB, PROBES, BS), jnp.float32).at[pair_rows].add(local_terms)
        sources = jnp.arange(N_WIDE)
        far_blocks = (sources[:, None] * N_NARROW + narrow_index) * NB + send_list[:, narrow_index, wide_index, :]
        far_blocks = far_blocks.reshape(-1)
        far_rows = target_list[wide_index, narrow_index].reshape(-1)
        far_terms = tile_product(own_sites[far_rows], coords[far_blocks], probe_half[far_blocks])
        return summed.at[far_rows].add(far_terms)
    kernel_rows = lax.map(per_device, jnp.arange(N_WIDE * N_NARROW, dtype=jnp.int32))
    applied = nugget * probe + kernel_rows.reshape(BLOCKS, PROBES, BS)
    directions = jnp.concatenate([probe, kept], axis=1)
    projections = jnp.einsum('bjs,bks->jk', directions, applied, precision=lax.Precision.HIGHEST) / SITES
    fresh = applied - jnp.einsum('bjs,jk->bks', directions, projections, precision=lax.Precision.HIGHEST)
    col_power = lax.optimization_barrier(jnp.sum(fresh * fresh, axis=(0, 2))) / SITES
    next_block = fresh / jnp.sqrt(col_power + eps)[None, :, None]
    return (next_block, projections)
```

```python
import functools

import jax
import jax.numpy as jnp
from jax import lax
from jax.experimental import pallas as pl
from jax.experimental.pallas import tpu as pltpu
from jax.sharding import PartitionSpec as P

MESH = pl.DeviceIdType.MESH

HALO = 2
TURN = 4
rho = 0.35
nugget = 1.0
eps = 1e-06

NT = (((1,), (1,)), ((), ()))
NN = (((1,), (0,)), ((), ()))


def split3(x):
    high = x.astype(jnp.bfloat16).astype(jnp.float32)
    rest = x - high
    mid = rest.astype(jnp.bfloat16).astype(jnp.float32)
    return high, mid, rest - mid


def norm_parts(sites):
    squared = jnp.sum(sites * sites, axis=0, keepdims=True) * (1.0 / rho**2)
    return split3(jnp.broadcast_to(squared, sites.shape))


def row_features(sites):
    high, mid, low = norm_parts(sites)
    place = lax.broadcasted_iota(jnp.int32, sites.shape, 0)
    tail = jnp.where(place < 3, 1.0, jnp.where(place == 3, high, jnp.where(place == 4, mid, low)))
    tail = jnp.where(place < 6, tail, 0.0)
    return jnp.concatenate([sites, sites, sites, tail], axis=0).astype(jnp.bfloat16)


def col_features(sites):
    high, mid, low = norm_parts(sites)
    place = lax.broadcasted_iota(jnp.int32, sites.shape, 0)
    tail = jnp.where(place == 0, high, jnp.where(place == 1, mid, jnp.where(place == 2, low, 1.0)))
    tail = jnp.where(place < 6, tail, 0.0)
    parts = split3(sites * (-2.0 / rho**2))
    return jnp.concatenate([*parts, tail], axis=0).T.astype(jnp.bfloat16)


def covariance(col_feat, row_feat):
    scaled2 = lax.dot_general(col_feat, row_feat, NN, preferred_element_type=jnp.float32)
    scaled2 = jnp.maximum(scaled2, 1e-12)
    support = jnp.maximum(1.0 - scaled2 * lax.rsqrt(scaled2), 0.0)
    square = support * support
    return (square * square * (1.25 - support)).astype(jnp.bfloat16)


def body(
    nw, nn,
    coords_ref, probe_ref, kept_ref, pairs_ref, counts_ref, send_ref, target_ref,
    next_ref, proj_ref,
    own, halo, stage, far, row_feat, col_feat, twice, masks, acc, split, part_w, part_n,
    halo_send, halo_recv, far_send, far_recv, pw_send, pw_recv, pn_send, pn_recv,
):
    w = lax.axis_index("wide")
    n = lax.axis_index("narrow")
    nb, probes, bs = probe_ref.shape
    basis = probes + kept_ref.shape[1]
    slots = send_ref.shape[3]
    pair_max = pairs_ref.shape[2]
    total_sites = float(nb * bs * nw * nn)

    barrier = pltpu.get_barrier_semaphore()
    for k in range(1, nw):
        pl.semaphore_signal(barrier, inc=1, device_id={"wide": lax.rem(w + k, nw)}, device_id_type=MESH)
    for k in range(1, nn):
        pl.semaphore_signal(barrier, inc=1, device_id={"narrow": lax.rem(n + k, nn)}, device_id_type=MESH)

    for b in range(nb):
        sites = jnp.concatenate(
            [coords_ref[b].astype(jnp.float32), jnp.zeros((8 - coords_ref.shape[1], bs), jnp.float32)], axis=0
        )
        own[b] = jnp.concatenate([sites, probe_ref[b]], axis=0).astype(jnp.bfloat16)

    for k in range(nw):
        w2 = lax.rem(w + k, nw)
        for s in range(slots):
            block = own[send_ref[0, 0, w2, s]]
            if k == 0:
                far[s] = block
            else:
                stage[k - 1, s] = block

    pl.semaphore_wait(barrier, nw + nn - 2)

    def far_copy(k):
        return pltpu.make_async_remote_copy(
            src_ref=stage.at[k - 1], dst_ref=far.at[pl.ds(k * slots, slots)],
            send_sem=far_send.at[k - 1], recv_sem=far_recv.at[k - 1],
            device_id={"wide": lax.rem(w + k, nw)}, device_id_type=MESH,
        )

    def up_copy():
        return pltpu.make_async_remote_copy(
            src_ref=own.at[pl.ds(nb - HALO, HALO)], dst_ref=halo.at[pl.ds(0, HALO)],
            send_sem=halo_send.at[0], recv_sem=halo_recv.at[0],
            device_id={"narrow": jnp.minimum(n + 1, nn - 1)}, device_id_type=MESH,
        )

    def down_copy():
        return pltpu.make_async_remote_copy(
            src_ref=own.at[pl.ds(0, HALO)], dst_ref=halo.at[pl.ds(HALO, HALO)],
            send_sem=halo_send.at[1], recv_sem=halo_recv.at[1],
            device_id={"narrow": jnp.maximum(n - 1, 0)}, device_id_type=MESH,
        )

    @pl.when(n < nn - 1)
    def _():
        up_copy().start()

    @pl.when(n > 0)
    def _():
        down_copy().start()

    for k in range(1, nw):
        far_copy(k).start()

    @pl.when(n == 0)
    def _():
        halo[0:HALO] = jnp.zeros((HALO,) + halo.shape[1:], halo.dtype)

    @pl.when(n == nn - 1)
    def _():
        halo[HALO:] = jnp.zeros((HALO,) + halo.shape[1:], halo.dtype)

    gram = jnp.zeros((3 * basis, basis), jnp.float32)
    for b in range(nb):
        parts = split3(jnp.concatenate([probe_ref[b], kept_ref[b]], axis=0))
        parts = [part.astype(jnp.bfloat16) for part in parts]
        stacked = jnp.concatenate(parts, axis=0)
        split[b] = stacked
        for part in parts:
            gram += lax.dot_general(stacked, part, NT, preferred_element_type=jnp.float32)
    gram = gram[2 * basis:] + gram[basis:2 * basis] + gram[:basis]

    mask_row = lax.broadcasted_iota(jnp.int32, (nb * probes, bs), 0) // probes
    for a in range(nb + 1):
        masks[a] = jnp.where(mask_row == a, 1.0, 0.0).astype(jnp.bfloat16)

    def prepare(slot, block):
        packed = block.astype(jnp.float32)
        col_feat[slot] = col_features(packed[:8])
        twice[slot] = jnp.concatenate([packed[8:], packed[8:]], axis=0).astype(jnp.bfloat16)
        return packed[:8]

    for b in range(nb):
        row_feat[b] = row_features(prepare(HALO + b, own[b]))

    acc[...] = nugget * probe_ref[...].reshape(nb * probes, bs)

    @pl.when(n > 0)
    def _():
        up_copy().wait_recv()

    @pl.when(n < nn - 1)
    def _():
        down_copy().wait_recv()

    for h in range(HALO):
        prepare(h, halo[h])
        prepare(HALO + nb + h, halo[HALO + h])

    def left(mask, probe2):
        return (mask.reshape(-1, 16, bs) * probe2[None]).reshape(mask.shape)

    count = counts_ref[0, 0]

    def local_turn(turn, carry):
        lefts, tiles = [], []
        for u in range(TURN):
            p = turn * TURN + u
            row = pairs_ref[0, 0, p, 0]
            slot = pairs_ref[0, 0, p, 1]
            within = n * nb - HALO + slot
            live = (p < count) & (within >= 0) & (within < nn * nb)
            lefts.append(left(masks[jnp.where(live, row, nb)], twice[slot]))
            tiles.append(covariance(col_feat[slot], row_feat[row]))
        acc[...] += lax.dot_general(
            jnp.concatenate(lefts, axis=1), jnp.concatenate(tiles, axis=0), NN,
            preferred_element_type=jnp.float32,
        )
        return carry

    lax.fori_loop(0, pair_max // TURN, local_turn, 0)

    for k in range(1, nw):
        far_copy(k).wait_recv()

    def far_turn(turn, carry):
        lefts, tiles = [], []
        for u in range(TURN):
            p = turn * TURN + u
            row = target_ref[0, 0, lax.rem(w - p // slots + nw, nw), p % slots]
            packed = far[p].astype(jnp.float32)
            probe2 = jnp.concatenate([packed[8:], packed[8:]], axis=0).astype(jnp.bfloat16)
            lefts.append(left(masks[row], probe2))
            tiles.append(covariance(col_features(packed[:8]), row_feat[row]))
        acc[...] += lax.dot_general(
            jnp.concatenate(lefts, axis=1), jnp.concatenate(tiles, axis=0), NN,
            preferred_element_type=jnp.float32,
        )
        return carry

    lax.fori_loop(0, nw * slots // TURN, far_turn, 0)

    inner = jnp.zeros((4 * probes, 4 * probes), jnp.float32)
    nothing = jnp.zeros((probes, bs), jnp.float32)
    for b in range(nb):
        high, mid, low = split3(acc[b * probes:(b + 1) * probes])
        first = jnp.concatenate([high, mid], axis=0).astype(jnp.bfloat16)
        second = jnp.concatenate([low, nothing], axis=0).astype(jnp.bfloat16)
        lhs = jnp.concatenate([first, second], axis=0)
        for u, part in enumerate((high, mid, low)):
            rhs = jnp.concatenate(
                [split[b, u * basis:(u + 1) * basis],
                 jnp.concatenate([part, nothing], axis=0).astype(jnp.bfloat16)], axis=0
            )
            inner += lax.dot_general(lhs, rhs, NT, preferred_element_type=jnp.float32)
    inner = inner[2 * probes:3 * probes] + inner[probes:2 * probes] + inner[:probes]
    inner = jnp.concatenate([inner, jnp.zeros((probes, 128 - inner.shape[1]), jnp.float32)], axis=1)
    gram = jnp.concatenate([gram, jnp.zeros((basis, 128 - basis), jnp.float32)], axis=1)

    def reduce(buf, axis, me, count, send, recv, value):
        buf[me] = value
        for k in range(1, count):
            pltpu.make_async_remote_copy(
                src_ref=buf.at[me], dst_ref=buf.at[me], send_sem=send.at[k - 1], recv_sem=recv.at[me],
                device_id={axis: lax.rem(me + k, count)}, device_id_type=MESH,
            ).start()
        for k in range(1, count):
            src = lax.rem(me + k, count)
            pltpu.make_async_remote_copy(
                src_ref=buf.at[src], dst_ref=buf.at[src], send_sem=send.at[k - 1], recv_sem=recv.at[src],
                device_id={axis: src}, device_id_type=MESH,
            ).wait_recv()
        total = buf[0]
        for k in range(1, count):
            total = total + buf[k]
        return total

    value = jnp.concatenate([inner, gram], axis=0)
    value = reduce(part_w, "wide", w, nw, pw_send, pw_recv, value)
    value = reduce(part_n, "narrow", n, nn, pn_send, pn_recv, value)

    raw = value[:probes]
    coef = raw * (1.0 / total_sites)
    lane = lax.broadcasted_iota(jnp.int32, raw.shape, 1)
    line = lax.broadcasted_iota(jnp.int32, raw.shape, 0)
    norm = jnp.sum(jnp.where(lane == line + basis, raw, 0.0), axis=1, keepdims=True)
    columns = [jnp.sum(jnp.where(lane == j, coef, 0.0), axis=1, keepdims=True) for j in range(basis)]
    coupled = jnp.zeros_like(raw)
    for j in range(basis):
        coupled = coupled + columns[j] * value[probes + j:probes + j + 1]
    quad = jnp.sum(jnp.where(lane < basis, coef * (coupled - 2.0 * raw), 0.0), axis=1, keepdims=True)
    power = jnp.maximum((norm + quad) * (1.0 / total_sites), 0.0)
    inv = 1.0 / jnp.sqrt(power + eps)
    proj_ref[...] = jnp.concatenate([coef] * (128 // probes), axis=0).T[:basis, :probes]
    for b in range(nb):
        fresh = acc[b * probes:(b + 1) * probes]
        for j in range(basis):
            source = probe_ref[b, j:j + 1] if j < probes else kept_ref[b, j - probes:j - probes + 1]
            fresh = fresh - columns[j] * source
        next_ref[b] = fresh * inv

    @pl.when(n < nn - 1)
    def _():
        up_copy().wait_send()

    @pl.when(n > 0)
    def _():
        down_copy().wait_send()

    for k in range(1, nw):
        far_copy(k).wait_send()
    for buf, axis, me, cnt, send, recv in (
        (part_w, "wide", w, nw, pw_send, pw_recv), (part_n, "narrow", n, nn, pn_send, pn_recv)
    ):
        for k in range(1, cnt):
            pltpu.make_async_remote_copy(
                src_ref=buf.at[me], dst_ref=buf.at[me], send_sem=send.at[k - 1], recv_sem=recv.at[me],
                device_id={axis: lax.rem(me + k, cnt)}, device_id_type=MESH,
            ).wait_send()


def solution(mesh):
    nw, nn = mesh.shape["wide"], mesh.shape["narrow"]

    def shards(coords, probe, kept, pairs, counts, send_list, target_list):
        nb, probes, bs = probe.shape
        basis = probes + kept.shape[1]
        slots = send_list.shape[3]
        bf16, f32 = jnp.bfloat16, jnp.float32
        vmem = pl.BlockSpec(memory_space=pltpu.VMEM)
        smem = pl.BlockSpec(memory_space=pltpu.SMEM)
        dma = pltpu.SemaphoreType.DMA
        return pl.pallas_call(
            functools.partial(body, nw, nn),
            out_shape=(
                jax.ShapeDtypeStruct((nb, probes, bs), f32),
                jax.ShapeDtypeStruct((basis, probes), f32),
            ),
            in_specs=[vmem] * 3 + [smem] * 4,
            out_specs=(vmem, vmem),
            scratch_shapes=[
                pltpu.VMEM((nb, 16, bs), bf16),
                pltpu.VMEM((2 * HALO, 16, bs), bf16),
                pltpu.VMEM((nw - 1, slots, 16, bs), bf16),
                pltpu.VMEM((nw * slots, 16, bs), bf16),
                pltpu.VMEM((nb, 32, bs), bf16),
                pltpu.VMEM((nb + 2 * HALO, bs, 32), bf16),
                pltpu.VMEM((nb + 2 * HALO, 16, bs), bf16),
                pltpu.VMEM((nb + 1, nb * probes, bs), bf16),
                pltpu.VMEM((nb * probes, bs), f32),
                pltpu.VMEM((nb, 3 * basis, bs), bf16),
                pltpu.VMEM((nw, probes + basis, 128), f32),
                pltpu.VMEM((nn, probes + basis, 128), f32),
                dma((2,)), dma((2,)),
                dma((nw - 1,)), dma((nw - 1,)),
                dma((nw - 1,)), dma((nw,)),
                dma((nn - 1,)), dma((nn,)),
            ],
            compiler_params=pltpu.CompilerParams(
                collective_id=0, has_side_effects=True, vmem_limit_bytes=32 * 2**20
            ),
            name="lanczos_step",
        )(coords, probe, kept, pairs, counts, send_list, target_list)

    blocks = P(("groups", "wide", "narrow"), None, None)
    lists = P(("groups", "wide"), "narrow", None, None)
    in_specs = (blocks, blocks, blocks, lists, P(("groups", "wide"), "narrow"), lists, lists)
    out_specs = (blocks, P("groups", None))
    return jax.shard_map(shards, mesh=mesh, in_specs=in_specs, out_specs=out_specs, check_vma=False)
```

```python
import functools

import jax
import jax.numpy as jnp
from jax import lax
from jax.experimental import pallas as pl
from jax.experimental.pallas import tpu as pltpu
from jax.sharding import PartitionSpec as P

MESH = pl.DeviceIdType.MESH

HALO = 2
TURN = 16
rho = 0.35
nugget = 1.0
eps = 1e-06

NT = (((1,), (1,)), ((), ()))
NN = (((1,), (0,)), ((), ()))


def split3(x):
    high = x.astype(jnp.bfloat16).astype(jnp.float32)
    rest = x - high
    mid = rest.astype(jnp.bfloat16).astype(jnp.float32)
    return high, mid, rest - mid


def norm_parts(sites):
    squared = jnp.sum(sites * sites, axis=0, keepdims=True) * (1.0 / rho**2)
    return split3(jnp.broadcast_to(squared, sites.shape))


def row_features(sites):
    high, mid, low = norm_parts(sites)
    place = lax.broadcasted_iota(jnp.int32, sites.shape, 0)
    tail = jnp.where(place < 3, 1.0, jnp.where(place == 3, high, jnp.where(place == 4, mid, low)))
    tail = jnp.where(place < 6, tail, 0.0)
    return jnp.concatenate([sites, sites, sites, tail], axis=0).astype(jnp.bfloat16)


def col_features(sites):
    high, mid, low = norm_parts(sites)
    place = lax.broadcasted_iota(jnp.int32, sites.shape, 0)
    tail = jnp.where(place == 0, high, jnp.where(place == 1, mid, jnp.where(place == 2, low, 1.0)))
    tail = jnp.where(place < 6, tail, 0.0)
    parts = split3(sites * (-2.0 / rho**2))
    return jnp.concatenate([*parts, tail], axis=0).T.astype(jnp.bfloat16)


def covariance(col_feat, row_feat):
    scaled2 = lax.dot_general(col_feat, row_feat, NN, preferred_element_type=jnp.float32)
    scaled2 = jnp.maximum(scaled2, 1e-12)
    support = jnp.maximum(1.0 - scaled2 * lax.rsqrt(scaled2), 0.0)
    square = support * support
    return (square * square * (1.25 - support)).astype(jnp.bfloat16)


def body(
    nw, nn,
    coords_hbm, probe_hbm, kept_hbm, pairs_hbm, counts_hbm, send_hbm, target_hbm,
    next_ref, proj_ref,
    coords_ref, probe_ref, kept_ref, pairs_ref, counts_ref, send_ref, target_ref, in_sem,
    own, halo, stage, far, row_feat, col_feat, twice, masks, acc, split, part_w, part_n,
    halo_send, halo_recv, far_send, far_recv, pw_send, pw_recv, pn_send, pn_recv,
):
    w = lax.axis_index("wide")
    n = lax.axis_index("narrow")
    nb, probes, bs = probe_ref.shape
    basis = probes + kept_ref.shape[1]
    slots = send_ref.shape[3]
    pair_max = pairs_ref.shape[3]
    total_sites = float(nb * bs * nw * nn)

    inputs = [
        pltpu.make_async_copy(src, dst, in_sem.at[place])
        for place, (src, dst) in enumerate((
            (coords_hbm, coords_ref), (probe_hbm, probe_ref), (send_hbm, send_ref), (kept_hbm, kept_ref),
            (target_hbm, target_ref), (pairs_hbm, pairs_ref), (counts_hbm, counts_ref),
        ))
    ]
    for copy in inputs:
        copy.start()

    barrier = pltpu.get_barrier_semaphore()
    for k in range(1, nw):
        pl.semaphore_signal(barrier, inc=1, device_id={"wide": lax.rem(w + k, nw)}, device_id_type=MESH)
    for k in range(1, nn):
        pl.semaphore_signal(barrier, inc=1, device_id={"narrow": lax.rem(n + k, nn)}, device_id_type=MESH)

    for copy in inputs[:3]:
        copy.wait()
    sites_all = coords_ref[...].astype(jnp.float32)
    site_line = lax.broadcasted_iota(jnp.int32, (8, bs), 0)
    for b in range(nb):
        sites = jnp.zeros((8, bs), jnp.float32)
        for component in range(sites_all.shape[0]):
            sites = jnp.where(site_line == component, sites_all[component, b:b + 1], sites)
        own[b] = jnp.concatenate([sites, probe_ref[b]], axis=0).astype(jnp.bfloat16)

    for k in range(nw):
        w2 = lax.rem(w + k, nw)
        for s in range(slots):
            block = own[send_ref[0, 0, w2, s]]
            if k == 0:
                far[s] = block
            else:
                stage[k - 1, s] = block

    pl.semaphore_wait(barrier, nw + nn - 2)

    def far_copy(k):
        return pltpu.make_async_remote_copy(
            src_ref=stage.at[k - 1], dst_ref=far.at[pl.ds(k * slots, slots)],
            send_sem=far_send.at[k - 1], recv_sem=far_recv.at[k - 1],
            device_id={"wide": lax.rem(w + k, nw)}, device_id_type=MESH,
        )

    def up_copy():
        return pltpu.make_async_remote_copy(
            src_ref=own.at[pl.ds(nb - HALO, HALO)], dst_ref=halo.at[pl.ds(0, HALO)],
            send_sem=halo_send.at[0], recv_sem=halo_recv.at[0],
            device_id={"narrow": jnp.minimum(n + 1, nn - 1)}, device_id_type=MESH,
        )

    def down_copy():
        return pltpu.make_async_remote_copy(
            src_ref=own.at[pl.ds(0, HALO)], dst_ref=halo.at[pl.ds(HALO, HALO)],
            send_sem=halo_send.at[1], recv_sem=halo_recv.at[1],
            device_id={"narrow": jnp.maximum(n - 1, 0)}, device_id_type=MESH,
        )

    @pl.when(n < nn - 1)
    def _():
        up_copy().start()

    @pl.when(n > 0)
    def _():
        down_copy().start()

    for k in range(1, nw):
        far_copy(k).start()

    @pl.when(n == 0)
    def _():
        halo[0:HALO] = jnp.zeros((HALO,) + halo.shape[1:], halo.dtype)

    @pl.when(n == nn - 1)
    def _():
        halo[HALO:] = jnp.zeros((HALO,) + halo.shape[1:], halo.dtype)

    mask_row = lax.broadcasted_iota(jnp.int32, (nb * probes, bs), 0) // probes
    for a in range(nb + 1):
        masks[a] = jnp.where(mask_row == a, 1.0, 0.0).astype(jnp.bfloat16)

    for copy in inputs[3:]:
        copy.wait()
    for b in range(nb):
        parts = split3(jnp.concatenate([probe_ref[b], kept_ref[b]], axis=0))
        stacked = jnp.concatenate([part.astype(jnp.bfloat16) for part in parts], axis=0)
        split[:, b * bs:(b + 1) * bs] = stacked
    gram = jnp.zeros((3 * basis, basis), jnp.float32)
    for u in range(3):
        gram += lax.dot_general(
            split[...], split[u * basis:(u + 1) * basis], NT, preferred_element_type=jnp.float32
        )
    gram = gram[2 * basis:] + gram[basis:2 * basis] + gram[:basis]

    def prepare(slot, block):
        packed = block.astype(jnp.float32)
        col_feat[slot] = col_features(packed[:8])
        twice[slot] = jnp.concatenate([packed[8:], packed[8:]], axis=0).astype(jnp.bfloat16)
        return packed[:8]

    for b in range(nb):
        row_feat[b] = row_features(prepare(HALO + b, own[b]))

    acc[...] = nugget * probe_ref[...].reshape(nb * probes, bs)

    def left(mask, probe2):
        return (mask.reshape(-1, 16, bs) * probe2[None]).reshape(mask.shape)

    def far_turn(first, size):
        lefts, tiles = [], []
        for u in range(size):
            p = first + u
            row = target_ref[0, 0, lax.rem(w - p // slots + nw, nw), p % slots]
            packed = far[p].astype(jnp.float32)
            probe2 = jnp.concatenate([packed[8:], packed[8:]], axis=0).astype(jnp.bfloat16)
            lefts.append(left(masks[row], probe2))
            tiles.append(covariance(col_features(packed[:8]), row_feat[row]))
        acc[...] += lax.dot_general(
            jnp.concatenate(lefts, axis=1), jnp.concatenate(tiles, axis=0), NN,
            preferred_element_type=jnp.float32,
        )

    far_turn(0, slots)

    @pl.when(n > 0)
    def _():
        up_copy().wait_recv()

    @pl.when(n < nn - 1)
    def _():
        down_copy().wait_recv()

    for h in range(HALO):
        prepare(h, halo[h])
        prepare(HALO + nb + h, halo[HALO + h])

    count = counts_ref[0, 0]

    def local_turn(turn, carry):
        lefts, tiles = [], []
        for u in range(TURN):
            p = turn * TURN + u
            row = pairs_ref[0, 0, 0, p]
            slot = pairs_ref[0, 0, 1, p]
            within = n * nb - HALO + slot
            live = (p < count) & (within >= 0) & (within < nn * nb)
            lefts.append(left(masks[jnp.where(live, row, nb)], twice[slot]))
            tiles.append(covariance(col_feat[slot], row_feat[row]))
        acc[...] += lax.dot_general(
            jnp.concatenate(lefts, axis=1), jnp.concatenate(tiles, axis=0), NN,
            preferred_element_type=jnp.float32,
        )
        return carry

    lax.fori_loop(0, pair_max // TURN, local_turn, 0)

    for k in range(1, nw):
        far_copy(k).wait_recv()

    def far_source(source, carry):
        far_turn(source * slots, slots)
        return carry

    lax.fori_loop(1, nw, far_source, 0)

    nothing = jnp.zeros((probes, bs), jnp.float32)
    lhs, rhs = [], [[], [], []]
    for b in range(nb):
        high, mid, low = split3(acc[b * probes:(b + 1) * probes])
        first = jnp.concatenate([high, mid], axis=0).astype(jnp.bfloat16)
        second = jnp.concatenate([low, nothing], axis=0).astype(jnp.bfloat16)
        lhs.append(jnp.concatenate([first, second], axis=0))
        for u, part in enumerate((high, mid, low)):
            rhs[u].append(jnp.concatenate([part, nothing], axis=0).astype(jnp.bfloat16))
    lhs = jnp.concatenate(lhs, axis=1)
    inner = jnp.zeros((4 * probes, 4 * probes), jnp.float32)
    for u in range(3):
        both = jnp.concatenate(
            [split[u * basis:(u + 1) * basis], jnp.concatenate(rhs[u], axis=1)], axis=0
        )
        inner += lax.dot_general(lhs, both, NT, preferred_element_type=jnp.float32)
    inner = inner[2 * probes:3 * probes] + inner[probes:2 * probes] + inner[:probes]
    inner = jnp.concatenate([inner, jnp.zeros((probes, 128 - inner.shape[1]), jnp.float32)], axis=1)
    gram = jnp.concatenate([gram, jnp.zeros((basis, 128 - basis), jnp.float32)], axis=1)

    def reduce(buf, axis, me, count, send, recv, value):
        buf[me] = value
        for k in range(1, count):
            pltpu.make_async_remote_copy(
                src_ref=buf.at[me], dst_ref=buf.at[me], send_sem=send.at[k - 1], recv_sem=recv.at[me],
                device_id={axis: lax.rem(me + k, count)}, device_id_type=MESH,
            ).start()
        for k in range(1, count):
            src = lax.rem(me + k, count)
            pltpu.make_async_remote_copy(
                src_ref=buf.at[src], dst_ref=buf.at[src], send_sem=send.at[k - 1], recv_sem=recv.at[src],
                device_id={axis: src}, device_id_type=MESH,
            ).wait_recv()
        total = buf[0]
        for k in range(1, count):
            total = total + buf[k]
        return total

    value = jnp.concatenate([inner, gram], axis=0)
    value = reduce(part_w, "wide", w, nw, pw_send, pw_recv, value)
    value = reduce(part_n, "narrow", n, nn, pn_send, pn_recv, value)

    raw = value[:probes]
    coef = raw * (1.0 / total_sites)
    lane = lax.broadcasted_iota(jnp.int32, raw.shape, 1)
    line = lax.broadcasted_iota(jnp.int32, raw.shape, 0)
    norm = jnp.sum(jnp.where(lane == line + basis, raw, 0.0), axis=1, keepdims=True)
    columns = [jnp.sum(jnp.where(lane == j, coef, 0.0), axis=1, keepdims=True) for j in range(basis)]
    coupled = jnp.zeros_like(raw)
    for j in range(basis):
        coupled = coupled + columns[j] * value[probes + j:probes + j + 1]
    quad = jnp.sum(jnp.where(lane < basis, coef * (coupled - 2.0 * raw), 0.0), axis=1, keepdims=True)
    power = jnp.maximum((norm + quad) * (1.0 / total_sites), 0.0)
    inv = 1.0 / jnp.sqrt(power + eps)
    proj_ref[...] = coef[:, :basis]
    for b in range(nb):
        fresh = acc[b * probes:(b + 1) * probes]
        for j in range(basis):
            source = probe_ref[b, j:j + 1] if j < probes else kept_ref[b, j - probes:j - probes + 1]
            fresh = fresh - columns[j] * source
        next_ref[b] = fresh * inv

    @pl.when(n < nn - 1)
    def _():
        up_copy().wait_send()

    @pl.when(n > 0)
    def _():
        down_copy().wait_send()

    for k in range(1, nw):
        far_copy(k).wait_send()
    for buf, axis, me, cnt, send, recv in (
        (part_w, "wide", w, nw, pw_send, pw_recv), (part_n, "narrow", n, nn, pn_send, pn_recv)
    ):
        for k in range(1, cnt):
            pltpu.make_async_remote_copy(
                src_ref=buf.at[me], dst_ref=buf.at[me], send_sem=send.at[k - 1], recv_sem=recv.at[me],
                device_id={axis: lax.rem(me + k, cnt)}, device_id_type=MESH,
            ).wait_send()


def solution(mesh):
    nw, nn = mesh.shape["wide"], mesh.shape["narrow"]

    def shards(coords, probe, kept, pairs, counts, send_list, target_list):
        nb, probes, bs = probe.shape
        basis = probes + kept.shape[1]
        slots = send_list.shape[3]
        bf16, f32 = jnp.bfloat16, jnp.float32
        vmem = pl.BlockSpec(memory_space=pltpu.VMEM)
        dma = pltpu.SemaphoreType.DMA
        next_block, coupled = pl.pallas_call(
            functools.partial(body, nw, nn),
            out_shape=(
                jax.ShapeDtypeStruct((nb, probes, bs), f32),
                jax.ShapeDtypeStruct((probes, basis), f32),
            ),
            in_specs=[pl.BlockSpec(memory_space=pl.ANY)] * 7,
            out_specs=(vmem, vmem),
            scratch_shapes=[
                pltpu.VMEM((coords.shape[1], nb, bs), bf16),
                pltpu.VMEM(probe.shape, f32),
                pltpu.VMEM(kept.shape, f32),
                pltpu.SMEM((1, 1, 2, pairs.shape[2]), jnp.int32),
                pltpu.SMEM(counts.shape, jnp.int32),
                pltpu.SMEM(send_list.shape, jnp.int32),
                pltpu.SMEM(target_list.shape, jnp.int32),
                dma((7,)),
                pltpu.VMEM((nb, 16, bs), bf16),
                pltpu.VMEM((2 * HALO, 16, bs), bf16),
                pltpu.VMEM((nw - 1, slots, 16, bs), bf16),
                pltpu.VMEM((nw * slots, 16, bs), bf16),
                pltpu.VMEM((nb, 32, bs), bf16),
                pltpu.VMEM((nb + 2 * HALO, bs, 32), bf16),
                pltpu.VMEM((nb + 2 * HALO, 16, bs), bf16),
                pltpu.VMEM((nb + 1, nb * probes, bs), bf16),
                pltpu.VMEM((nb * probes, bs), f32),
                pltpu.VMEM((3 * basis, nb * bs), bf16),
                pltpu.VMEM((nw, probes + basis, 128), f32),
                pltpu.VMEM((nn, probes + basis, 128), f32),
                dma((2,)), dma((2,)),
                dma((nw - 1,)), dma((nw - 1,)),
                dma((nw - 1,)), dma((nw,)),
                dma((nn - 1,)), dma((nn,)),
            ],
            compiler_params=pltpu.CompilerParams(
                collective_id=0, has_side_effects=True, vmem_limit_bytes=56 * 2**20
            ),
            name="lanczos_step",
        )(
            coords.transpose(1, 0, 2), probe, kept, pairs.transpose(0, 1, 3, 2), counts, send_list, target_list
        )
        return next_block, coupled.T

    blocks = P(("groups", "wide", "narrow"), None, None)
    lists = P(("groups", "wide"), "narrow", None, None)
    in_specs = (blocks, blocks, blocks, lists, P(("groups", "wide"), "narrow"), lists, lists)
    out_specs = (blocks, P("groups", None))
    return jax.shard_map(shards, mesh=mesh, in_specs=in_specs, out_specs=out_specs, check_vma=False)
```

```python
import functools

import jax
import jax.numpy as jnp
from jax import lax
from jax.experimental import pallas as pl
from jax.experimental.pallas import tpu as pltpu
from jax.sharding import PartitionSpec as P

MESH = pl.DeviceIdType.MESH

HALO = 2
TURN = 32
rho = 0.35
nugget = 1.0
eps = 1e-06

NT = (((1,), (1,)), ((), ()))
NN = (((1,), (0,)), ((), ()))


def split3(x):
    high = x.astype(jnp.bfloat16).astype(jnp.float32)
    rest = x - high
    mid = rest.astype(jnp.bfloat16).astype(jnp.float32)
    return high, mid, rest - mid


def norm_parts(sites):
    squared = jnp.sum(sites * sites, axis=0, keepdims=True) * (1.0 / rho**2)
    return split3(jnp.broadcast_to(squared, sites.shape))


def row_features(sites):
    high, mid, low = norm_parts(sites)
    place = lax.broadcasted_iota(jnp.int32, sites.shape, 0)
    tail = jnp.where(place < 3, 1.0, jnp.where(place == 3, high, jnp.where(place == 4, mid, low)))
    tail = jnp.where(place < 6, tail, 0.0)
    return jnp.concatenate([sites, sites, sites, tail], axis=0).astype(jnp.bfloat16)


def col_features(sites):
    high, mid, low = norm_parts(sites)
    place = lax.broadcasted_iota(jnp.int32, sites.shape, 0)
    tail = jnp.where(place == 0, high, jnp.where(place == 1, mid, jnp.where(place == 2, low, 1.0)))
    tail = jnp.where(place < 6, tail, 0.0)
    parts = split3(sites * (-2.0 / rho**2))
    return jnp.concatenate([*parts, tail], axis=0).T.astype(jnp.bfloat16)


def covariance(col_feat, row_feat):
    scaled2 = lax.dot_general(col_feat, row_feat, NN, preferred_element_type=jnp.float32)
    scaled2 = jnp.maximum(scaled2, 1e-12)
    support = jnp.maximum(1.0 - scaled2 * lax.rsqrt(scaled2), 0.0)
    square = support * support
    return (square * square * (1.25 - support)).astype(jnp.bfloat16)


def body(
    nw, nn,
    coords_hbm, probe_hbm, kept_hbm, pairs_hbm, counts_hbm, send_hbm, target_hbm,
    next_ref, proj_ref,
    coords_ref, probe_ref, kept_ref, pairs_ref, counts_ref, send_ref, target_ref, in_sem,
    own, halo, stage, far, row_feat, col_feat, twice, masks, acc, split, gram_w, gram_n, last_w, last_n, last_all,
    halo_send, halo_recv, far_send, far_recv, gw_send, gw_recv, gn_send, gn_recv,
    lw_send, lw_recv, ln_send, ln_recv, la_send, la_recv,
):
    w = lax.axis_index("wide")
    n = lax.axis_index("narrow")
    nb, probes, bs = probe_ref.shape
    basis = probes + kept_ref.shape[1]
    slots = send_ref.shape[3]
    pair_max = pairs_ref.shape[3]
    total_sites = float(nb * bs * nw * nn)

    def along_wide(k):
        return {"wide": lax.rem(w + k, nw)}

    def along_narrow(k):
        return {"narrow": lax.rem(n + k, nn)}

    def along_both(k):
        return {"wide": lax.rem(w + k // nn, nw), "narrow": lax.rem(n + k % nn, nn)}

    direct = nw * nn <= 32
    if direct:
        partners = [along_both(k) for k in range(1, nw * nn)]
    else:
        partners = [along_wide(k) for k in range(1, nw)] + [along_narrow(k) for k in range(1, nn)]

    inputs = [
        pltpu.make_async_copy(src, dst, in_sem.at[place])
        for place, (src, dst) in enumerate((
            (coords_hbm, coords_ref), (probe_hbm, probe_ref), (send_hbm, send_ref), (kept_hbm, kept_ref),
            (target_hbm, target_ref), (pairs_hbm, pairs_ref), (counts_hbm, counts_ref),
        ))
    ]
    for copy in inputs:
        copy.start()

    barrier = pltpu.get_barrier_semaphore()
    for device in partners:
        pl.semaphore_signal(barrier, inc=1, device_id=device, device_id_type=MESH)

    mask_row = lax.broadcasted_iota(jnp.int32, (nb * probes, bs), 0) // probes
    for a in range(nb + 1):
        masks[a] = jnp.where(mask_row == a, 1.0, 0.0).astype(jnp.bfloat16)

    @pl.when(n == 0)
    def _():
        halo[0:HALO] = jnp.zeros((HALO,) + halo.shape[1:], halo.dtype)

    @pl.when(n == nn - 1)
    def _():
        halo[HALO:] = jnp.zeros((HALO,) + halo.shape[1:], halo.dtype)

    for copy in inputs[:3]:
        copy.wait()
    sites_all = coords_ref[...].astype(jnp.float32)
    site_line = lax.broadcasted_iota(jnp.int32, (8, bs), 0)
    for b in range(nb):
        sites = jnp.zeros((8, bs), jnp.float32)
        for component in range(sites_all.shape[0]):
            sites = jnp.where(site_line == component, sites_all[component, b:b + 1], sites)
        own[b] = jnp.concatenate([sites, probe_ref[b]], axis=0).astype(jnp.bfloat16)

    for k in range(nw):
        w2 = lax.rem(w + k, nw)
        for s in range(slots):
            block = own[send_ref[0, 0, w2, s]]
            if k == 0:
                far[s] = block
            else:
                stage[k - 1, s] = block

    pl.semaphore_wait(barrier, len(partners))

    def far_copy(k):
        return pltpu.make_async_remote_copy(
            src_ref=stage.at[k - 1], dst_ref=far.at[pl.ds(k * slots, slots)],
            send_sem=far_send.at[k - 1], recv_sem=far_recv.at[k - 1],
            device_id={"wide": lax.rem(w + k, nw)}, device_id_type=MESH,
        )

    def up_copy():
        return pltpu.make_async_remote_copy(
            src_ref=own.at[pl.ds(nb - HALO, HALO)], dst_ref=halo.at[pl.ds(0, HALO)],
            send_sem=halo_send.at[0], recv_sem=halo_recv.at[0],
            device_id={"narrow": jnp.minimum(n + 1, nn - 1)}, device_id_type=MESH,
        )

    def down_copy():
        return pltpu.make_async_remote_copy(
            src_ref=own.at[pl.ds(0, HALO)], dst_ref=halo.at[pl.ds(HALO, HALO)],
            send_sem=halo_send.at[1], recv_sem=halo_recv.at[1],
            device_id={"narrow": jnp.maximum(n - 1, 0)}, device_id_type=MESH,
        )

    @pl.when(n < nn - 1)
    def _():
        up_copy().start()

    @pl.when(n > 0)
    def _():
        down_copy().start()

    for k in range(1, nw):
        far_copy(k).start()

    def exchange(buf, send, recv, device_of, me, count):
        def copies():
            return [
                pltpu.make_async_remote_copy(
                    src_ref=buf.at[me], dst_ref=buf.at[me], send_sem=send.at[k - 1], recv_sem=recv.at[me],
                    device_id=device_of(k), device_id_type=MESH,
                )
                for k in range(1, count)
            ]

        def start(value):
            buf[me] = value
            for copy in copies():
                copy.start()

        def finish(source_of):
            for k in range(1, count):
                source = source_of(k)
                pltpu.make_async_remote_copy(
                    src_ref=buf.at[source], dst_ref=buf.at[source], send_sem=send.at[k - 1],
                    recv_sem=recv.at[source], device_id=device_of(k), device_id_type=MESH,
                ).wait_recv()
            terms = [buf[k] for k in range(count)]
            while len(terms) > 1:
                terms = [sum(terms[k + 1:k + 2], terms[k]) for k in range(0, len(terms), 2)]
            return terms[0]

        def drain():
            for copy in copies():
                copy.wait_send()

        return start, finish, drain

    def wide_source(k):
        return lax.rem(w + k, nw)

    def narrow_source(k):
        return lax.rem(n + k, nn)

    def both_source(k):
        return lax.rem(w + k // nn, nw) * nn + lax.rem(n + k % nn, nn)

    gram_wide = exchange(gram_w, gw_send, gw_recv, along_wide, w, nw)
    gram_narrow = exchange(gram_n, gn_send, gn_recv, along_narrow, n, nn)
    last_wide = exchange(last_w, lw_send, lw_recv, along_wide, w, nw)
    last_narrow = exchange(last_n, ln_send, ln_recv, along_narrow, n, nn)
    last_both = exchange(last_all, la_send, la_recv, along_both, w * nn + n, nw * nn if direct else 1)

    for copy in inputs[3:]:
        copy.wait()
    for b in range(nb):
        parts = split3(jnp.concatenate([probe_ref[b], kept_ref[b]], axis=0))
        stacked = jnp.concatenate([part.astype(jnp.bfloat16) for part in parts], axis=0)
        split[:, b * bs:(b + 1) * bs] = stacked
    gram = jnp.zeros((3 * basis, basis), jnp.float32)
    for u in range(3):
        gram += lax.dot_general(
            split[...], split[u * basis:(u + 1) * basis], NT, preferred_element_type=jnp.float32
        )
    gram = gram[2 * basis:] + gram[basis:2 * basis] + gram[:basis]
    gram_wide[0](jnp.concatenate([gram, jnp.zeros((basis, 128 - basis), jnp.float32)], axis=1))

    def prepare(slot, block):
        packed = block.astype(jnp.float32)
        col_feat[slot] = col_features(packed[:8])
        twice[slot] = jnp.concatenate([packed[8:], packed[8:]], axis=0).astype(jnp.bfloat16)
        return packed[:8]

    for b in range(nb):
        row_feat[b] = row_features(prepare(HALO + b, own[b]))

    acc[...] = nugget * probe_ref[...].reshape(nb * probes, bs)

    def left(mask, probe2):
        return (mask.reshape(-1, 16, bs) * probe2[None]).reshape(mask.shape)

    def far_turn(first, size):
        lefts, tiles = [], []
        for u in range(size):
            p = first + u
            row = target_ref[0, 0, lax.rem(w - p // slots + nw, nw), p % slots]
            packed = far[p].astype(jnp.float32)
            probe2 = jnp.concatenate([packed[8:], packed[8:]], axis=0).astype(jnp.bfloat16)
            lefts.append(left(masks[row], probe2))
            tiles.append(covariance(col_features(packed[:8]), row_feat[row]))
        acc[...] += lax.dot_general(
            jnp.concatenate(lefts, axis=1), jnp.concatenate(tiles, axis=0), NN,
            preferred_element_type=jnp.float32,
        )

    far_turn(0, slots)

    @pl.when(n > 0)
    def _():
        up_copy().wait_recv()

    @pl.when(n < nn - 1)
    def _():
        down_copy().wait_recv()

    for h in range(HALO):
        prepare(h, halo[h])
        prepare(HALO + nb + h, halo[HALO + h])

    count = counts_ref[0, 0]

    def local_turn(turn, carry):
        lefts, tiles = [], []
        for u in range(TURN):
            p = turn * TURN + u
            row = pairs_ref[0, 0, 0, p]
            slot = pairs_ref[0, 0, 1, p]
            within = n * nb - HALO + slot
            live = (p < count) & (within >= 0) & (within < nn * nb)
            lefts.append(left(masks[jnp.where(live, row, nb)], twice[slot]))
            tiles.append(covariance(col_feat[slot], row_feat[row]))
        acc[...] += lax.dot_general(
            jnp.concatenate(lefts, axis=1), jnp.concatenate(tiles, axis=0), NN,
            preferred_element_type=jnp.float32,
        )
        return carry

    lax.fori_loop(0, pair_max // TURN, local_turn, 0)
    gram_narrow[0](gram_wide[1](wide_source))

    for k in range(1, nw):
        far_copy(k).wait_recv()

    def far_source(source, carry):
        far_turn(source * slots, slots)
        return carry

    if nw <= 4:
        far_turn(slots, (nw - 1) * slots)
    else:
        lax.fori_loop(1, nw, far_source, 0)

    nothing = jnp.zeros((probes, bs), jnp.float32)
    lhs, rhs = [], [[], [], []]
    for b in range(nb):
        high, mid, low = split3(acc[b * probes:(b + 1) * probes])
        first = jnp.concatenate([high, mid], axis=0).astype(jnp.bfloat16)
        second = jnp.concatenate([low, nothing], axis=0).astype(jnp.bfloat16)
        lhs.append(jnp.concatenate([first, second], axis=0))
        for u, part in enumerate((high, mid, low)):
            rhs[u].append(jnp.concatenate([part, nothing], axis=0).astype(jnp.bfloat16))
    lhs = jnp.concatenate(lhs, axis=1)
    inner = jnp.zeros((4 * probes, 4 * probes), jnp.float32)
    for u in range(3):
        both = jnp.concatenate(
            [split[u * basis:(u + 1) * basis], jnp.concatenate(rhs[u], axis=1)], axis=0
        )
        inner += lax.dot_general(lhs, both, NT, preferred_element_type=jnp.float32)
    inner = inner[2 * probes:3 * probes] + inner[probes:2 * probes] + inner[:probes]
    inner = jnp.concatenate([inner, jnp.zeros((probes, 128 - inner.shape[1]), jnp.float32)], axis=1)
    if direct:
        last_both[0](inner)
        gram = gram_narrow[1](narrow_source)
        raw = last_both[1](both_source)
    else:
        last_wide[0](inner)
        gram = gram_narrow[1](narrow_source)
        last_narrow[0](last_wide[1](wide_source))
        raw = last_narrow[1](narrow_source)
    coef = raw * (1.0 / total_sites)
    lane = lax.broadcasted_iota(jnp.int32, raw.shape, 1)
    line = lax.broadcasted_iota(jnp.int32, raw.shape, 0)
    norm = jnp.sum(jnp.where(lane == line + basis, raw, 0.0), axis=1, keepdims=True)
    columns = [jnp.sum(jnp.where(lane == j, coef, 0.0), axis=1, keepdims=True) for j in range(basis)]
    coupled = jnp.zeros_like(raw)
    for j in range(basis):
        coupled = coupled + columns[j] * gram[j:j + 1]
    quad = jnp.sum(jnp.where(lane < basis, coef * (coupled - 2.0 * raw), 0.0), axis=1, keepdims=True)
    power = jnp.maximum((norm + quad) * (1.0 / total_sites), 0.0)
    inv = 1.0 / jnp.sqrt(power + eps)
    proj_ref[...] = coef[:, :basis]
    for b in range(nb):
        fresh = acc[b * probes:(b + 1) * probes]
        for j in range(basis):
            source = probe_ref[b, j:j + 1] if j < probes else kept_ref[b, j - probes:j - probes + 1]
            fresh = fresh - columns[j] * source
        next_ref[b] = fresh * inv

    @pl.when(n < nn - 1)
    def _():
        up_copy().wait_send()

    @pl.when(n > 0)
    def _():
        down_copy().wait_send()

    for k in range(1, nw):
        far_copy(k).wait_send()
    gram_wide[2]()
    gram_narrow[2]()
    if direct:
        last_both[2]()
    else:
        last_wide[2]()
        last_narrow[2]()


def solution(mesh):
    nw, nn = mesh.shape["wide"], mesh.shape["narrow"]

    def shards(coords, probe, kept, pairs, counts, send_list, target_list):
        nb, probes, bs = probe.shape
        basis = probes + kept.shape[1]
        slots = send_list.shape[3]
        bf16, f32 = jnp.bfloat16, jnp.float32
        vmem = pl.BlockSpec(memory_space=pltpu.VMEM)
        dma = pltpu.SemaphoreType.DMA
        next_block, coupled = pl.pallas_call(
            functools.partial(body, nw, nn),
            out_shape=(
                jax.ShapeDtypeStruct((nb, probes, bs), f32),
                jax.ShapeDtypeStruct((probes, basis), f32),
            ),
            in_specs=[pl.BlockSpec(memory_space=pl.ANY)] * 7,
            out_specs=(vmem, vmem),
            scratch_shapes=[
                pltpu.VMEM((coords.shape[1], nb, bs), bf16),
                pltpu.VMEM(probe.shape, f32),
                pltpu.VMEM(kept.shape, f32),
                pltpu.SMEM((1, 1, 2, pairs.shape[2]), jnp.int32),
                pltpu.SMEM(counts.shape, jnp.int32),
                pltpu.SMEM(send_list.shape, jnp.int32),
                pltpu.SMEM(target_list.shape, jnp.int32),
                dma((7,)),
                pltpu.VMEM((nb, 16, bs), bf16),
                pltpu.VMEM((2 * HALO, 16, bs), bf16),
                pltpu.VMEM((nw - 1, slots, 16, bs), bf16),
                pltpu.VMEM((nw * slots, 16, bs), bf16),
                pltpu.VMEM((nb, 32, bs), bf16),
                pltpu.VMEM((nb + 2 * HALO, bs, 32), bf16),
                pltpu.VMEM((nb + 2 * HALO, 16, bs), bf16),
                pltpu.VMEM((nb + 1, nb * probes, bs), bf16),
                pltpu.VMEM((nb * probes, bs), f32),
                pltpu.VMEM((3 * basis, nb * bs), bf16),
                pltpu.VMEM((nw, basis, 128), f32),
                pltpu.VMEM((nn, basis, 128), f32),
                pltpu.VMEM((nw, probes, 128), f32),
                pltpu.VMEM((nn, probes, 128), f32),
                pltpu.VMEM((nw * nn, probes, 128), f32),
                dma((2,)), dma((2,)),
                dma((nw - 1,)), dma((nw - 1,)),
                dma((nw - 1,)), dma((nw,)),
                dma((nn - 1,)), dma((nn,)),
                dma((nw - 1,)), dma((nw,)),
                dma((nn - 1,)), dma((nn,)),
                dma((nw * nn - 1,)), dma((nw * nn,)),
            ],
            compiler_params=pltpu.CompilerParams(
                collective_id=0, has_side_effects=True, vmem_limit_bytes=56 * 2**20
            ),
            name="lanczos_step",
        )(
            coords.transpose(1, 0, 2), probe, kept, pairs.transpose(0, 1, 3, 2), counts, send_list, target_list
        )
        return next_block, coupled.T

    blocks = P(("groups", "wide", "narrow"), None, None)
    lists = P(("groups", "wide"), "narrow", None, None)
    in_specs = (blocks, blocks, blocks, lists, P(("groups", "wide"), "narrow"), lists, lists)
    out_specs = (blocks, P("groups", None))
    return jax.shard_map(shards, mesh=mesh, in_specs=in_specs, out_specs=out_specs, check_vma=False)
```
